512 devices in a mesh: area: 128 (over z, y, core), nrn: 4 (over x).
Axes of the slice: x: 4, y: 8, z: 8, core: 2. Of those that a mesh axis runs over, the one named last changes fastest.
Arguments:
- history: float32 [4, 65536, 128], P(None, ('area', 'nrn')), may hold values from -1 to 1
- drive: float32 [65536, 128], P(('area', 'nrn')), may hold values from -6 to 6
- leak: float32 [65536], P(('area', 'nrn')), may hold values from 0.1 to 0.9
- w_local: float32 [65536, 512], P(('area', 'nrn')), may hold values from -0.25 to 0.25
- w_long: float32 [65536, 4, 1152], P(('area', 'nrn')), may hold values from -0.1875 to 0.1875
- sender_rows: int32 [512, 128, 9], P(('area', 'nrn')), may hold values from 0 to 127
- delays: int32 [128, 128], P('area'), may hold values from 1 to 4
- area_sizes: int32 [128], P('area'), may hold values from 256 to 512, as said below
Outputs:
- rates: float32 [65536, 128], P(('area', 'nrn'))
The draws below stay inside these ranges and needn't reach their ends.
Inputs may be any that keep to these rules, and one draw needn't show every extreme that they name: `area_sizes`: every area has at least half of its 512 slots live; some area has all of them live, some exactly half. `sender_rows`: indices may repeat.
All inputs are finite; a program needn't handle non-finite values.
Results may differ from the reference program's by a relative error of at most 0.0018.
Values may be sent and summed in bfloat16 or wider, within the bound.
A program may use at most 64 MiB of HBM per device.

```python
import math
import jax
import jax.numpy as jnp
from jax import lax

BLK = 128
STIM = 128
PROJ_ROWS = 9
DMAX = 4
STEPS = 6
AREA_NEURONS = 512
BLOCKS = 512
NEURONS = 65536
N_AREA = 128
N_NRN = 4


def draw_area_sizes(key, part):
    first_key, second_key = jax.random.split(jax.random.fold_in(key, 11))
    sizes = jax.random.randint(first_key, (N_AREA,), AREA_NEURONS // 2, AREA_NEURONS + 1, dtype=jnp.int32)
    chosen = jax.random.randint(second_key, (), 0, N_AREA, dtype=jnp.int32)
    positions = jnp.arange(N_AREA, dtype=jnp.int32)
    sizes = jnp.where(positions == chosen, AREA_NEURONS, sizes)
    sizes = jnp.where(positions == (chosen + 1) % N_AREA, AREA_NEURONS // 2, sizes)
    return sizes.astype(jnp.int32)


def touch_ends(entries, key, smallest, high):
    longest = entries.shape.index(max(entries.shape))
    spots = []
    for shift in (0, 1):
        where = [jax.random.randint(jax.random.fold_in(key, axis), (), 0, length) for axis, length in enumerate(entries.shape)]
        where[longest] = (where[longest] + shift) % entries.shape[longest]
        spots.append(tuple(where))
    return entries.at[spots[0]].set(smallest).at[spots[1]].set(high)


def block_levels(rng, dims, cuts, low, high):
    loudness, own = 1.0, jax.random.fold_in(rng, 6)
    for position, blocks in cuts:
        heights = jnp.exp(jax.random.uniform(jax.random.fold_in(own, position), (blocks,), jnp.float32, low / len(cuts), high / len(cuts)))
        loudness = loudness * jnp.repeat(heights, dims[position] // blocks).reshape([-1 if axis == position else 1 for axis in range(len(dims))])
    return loudness


def gaussian(stream_key, dims, spread, reach, shards=(), held_as=jnp.bfloat16):
    entries = spread * jax.random.normal(stream_key, dims, jnp.float32)
    if shards:
        entries = entries * block_levels(stream_key, dims, shards, -0.22, 0.18)
    return jnp.clip(entries, -reach, reach).astype(held_as)


def setup_inputs(seed: int = 0) -> dict:
    key_list = jax.random.split(jax.random.key(seed), 9)
    return {
        "history": jnp.clip(jax.random.uniform(key_list[0], (DMAX, NEURONS, STIM), jnp.float32, -1.0, 1.0) * block_levels(key_list[0], (DMAX, NEURONS, STIM), ((1, 512),), -0.4, 0.0), -1.0, 1.0),
        "drive": gaussian(key_list[1], (NEURONS, STIM), 1.0, 6.0, ((0, 512),), jnp.float32),
        "leak": jnp.clip(jnp.exp(math.log(0.9) - 2.1972245 * jax.random.uniform(key_list[2], (NEURONS,), jnp.float32) ** block_levels(key_list[2], (NEURONS,), ((0, 512),), -0.2, 0.2)), 0.1, 0.9),
        "w_local": gaussian(key_list[3], (NEURONS, AREA_NEURONS), AREA_NEURONS ** -0.5, 0.25, ((0, 512),), jnp.float32),
        "w_long": gaussian(key_list[4], (NEURONS, N_NRN, N_AREA * PROJ_ROWS), (N_AREA * PROJ_ROWS) ** -0.5, 0.1875, ((0, 512),), jnp.float32),
        "sender_rows": touch_ends(jax.random.randint(key_list[5], (BLOCKS, N_AREA, PROJ_ROWS), 0, BLK), jax.random.fold_in(key_list[5], 1), 0, BLK - 1).astype(jnp.int32),
        "delays": touch_ends(jax.random.randint(key_list[6], (N_AREA, N_AREA), 1, DMAX + 1), jax.random.fold_in(key_list[6], 1), 1, DMAX).astype(jnp.int32),
        "area_sizes": draw_area_sizes(jax.random.fold_in(key_list[8], 71), 0),
    }


def unround(values):
    return lax.optimization_barrier(values).astype(jnp.float32)


def reference(history, drive, leak, w_local, w_long, sender_rows, delays, area_sizes):
    area_width = N_NRN * BLK
    neurons = history.shape[1]
    blocks = N_AREA * N_NRN
    positions = jnp.arange(neurons, dtype=jnp.int32)
    active = ((positions % area_width) < area_sizes[positions // area_width]).astype(jnp.float32)[:, None]
    states = history * active[None]
    block_ids = jnp.arange(blocks, dtype=jnp.int32)
    for iteration in range(STEPS):
        block_view = states.reshape(DMAX, blocks, BLK, STIM)
        current = unround(states[0].astype(jnp.bfloat16))

        def area_input(area_id):
            lagged = jnp.repeat(delays[:, area_id] - 1, N_NRN)
            chosen = sender_rows[:, area_id, :]
            gathered = block_view[lagged[:, None], block_ids[:, None], chosen]
            gathered = unround(gathered.astype(jnp.bfloat16))
            gathered = gathered.reshape(N_AREA, N_NRN, PROJ_ROWS, STIM).transpose(1, 0, 2, 3).reshape(-1, STIM)
            start = (area_id * area_width).astype(jnp.int32)
            weights = lax.dynamic_slice_in_dim(w_long, start, area_width, 0).reshape(area_width, -1)
            long_term = jnp.dot(weights, gathered, precision=lax.Precision.HIGHEST, preferred_element_type=jnp.float32)
            local_rows = lax.dynamic_slice_in_dim(current, start, area_width, 0)
            local_weights = lax.dynamic_slice_in_dim(w_local, start, area_width, 0)
            return long_term + jnp.dot(local_weights, local_rows, precision=lax.Precision.HIGHEST, preferred_element_type=jnp.float32)

        inputs = lax.map(area_input, jnp.arange(N_AREA, dtype=jnp.int32)).reshape(neurons, STIM) + drive
        updated = active * (states[0] + leak[:, None] * (jnp.tanh(inputs) - states[0]))
        states = jnp.concatenate([updated[None], states[:-1]], axis=0)
    return states[0]
```

```python
import jax
import jax.numpy as jnp
import numpy as np
from jax import lax
from jax.experimental import pallas as pl
from jax.experimental.pallas import tpu as pltpu
from jax.sharding import PartitionSpec as P

STEPS = 6
SIDE = 8
PEERS = 4
DEPTH = 4
ROWS = 128
PROJ = 9
SLOTS = 10
MSG = SLOTS * SIDE
CODES = 2 * SIDE * SLOTS
LONG = 2 * SIDE * MSG
ORDER = (4, 3, 5, 2, 6, 1, 7)
MESH = pl.DeviceIdType.MESH
F32 = jnp.float32
BF16 = jnp.bfloat16
UNITS = 32767.0 / 0.25


def kernel(
    history, drive, leak, sizes, table, w, out,
    tables, held, pick, mixed, msg, got, wg, halves, part, parts, rate, mask, pace,
    table_send, table_recv, first_send, first_recv, w_send, w_recv,
    hop1_send, hop1_recv, hop2_send, hop2_recv, x_send, x_recv,
):
    area = lax.axis_index("area")
    x = lax.axis_index("nrn")
    c = area % 2
    y = (area // 2) % SIDE
    z = area // (2 * SIDE)
    p = z + (y - z) * c
    s = y + (z - y) * c
    p_stride = 2 * SIDE + (2 - 2 * SIDE) * c
    s_stride = 2 + (2 * SIDE - 2) * c

    def at(pp, ss, cc):
        return pp * p_stride + ss * s_stride + cc

    def remote(src, dst, send, recv, target_area, target_x):
        return pltpu.make_async_remote_copy(
            src_ref=src, dst_ref=dst, send_sem=send, recv_sem=recv,
            device_id=(target_area, target_x), device_id_type=MESH,
        )

    def arrive(ref, recv):
        remote(ref, ref, recv, recv, area, x).wait_recv()

    near = [(p + r) % SIDE for r in ORDER]
    far = [(s + r) % SIDE for r in ORDER]
    every = [(p + r) % SIDE for r in (0,) + ORDER]
    across = [(x + r) % PEERS for r in (2, 1, 3)]

    barrier = pltpu.get_barrier_semaphore()
    for pp in near:
        pl.semaphore_signal(barrier, inc=1, device_id=(at(pp, s, c), x), device_id_type=MESH)
    for ss in far:
        pl.semaphore_signal(barrier, inc=1, device_id=(at(p, ss, c), x), device_id_type=MESH)
    for pp in every:
        pl.semaphore_signal(barrier, inc=1, device_id=(at(pp, s, 1 - c), x), device_id_type=MESH)
    for i in across:
        pl.semaphore_signal(barrier, inc=1, device_id=(area, i), device_id_type=MESH)

    alive = (lax.broadcasted_iota(jnp.int32, (ROWS, ROWS), 0) + x * ROWS < sizes[0]).astype(F32)
    mask[...] = alive
    pace[...] = jnp.broadcast_to(leak[...], (ROWS, ROWS)).T
    rate[...] = history[0] * alive
    for i in range(DEPTH):
        held[p, DEPTH - 1 - i] = (history[i] * alive).astype(BF16)
    tables[p] = table[...]

    pl.semaphore_wait(barrier, 2 * len(near) + len(every) + len(across))

    def table_copy(pp):
        return remote(table, tables.at[p], table_send.at[pp], table_recv.at[p], at(pp, s, c), x)

    def first_copy(pp):
        ref = held.at[p, pl.ds(0, DEPTH)]
        return remote(ref, ref, first_send.at[pp], first_recv.at[p], at(pp, s, c), x)

    def w_copy(i):
        return remote(w.at[i], wg.at[x], w_send.at[i], w_recv.at[x], area, i)

    def hop1_copy(t, pp):
        ref = held.at[p, t + DEPTH - 1]
        return remote(ref, ref, hop1_send.at[t, pp], hop1_recv.at[t, p], at(pp, s, c), x)

    def hop2_copy(t, ss, cc):
        a = ss * 2 + cc
        return remote(
            msg.at[t, a], got.at[t, c * SIDE + s], hop2_send.at[t, a], hop2_recv.at[t, c * SIDE + s], at(p, ss, cc), x
        )

    def x_copy(t, i):
        return remote(part.at[t, i], parts.at[t, x], x_send.at[t, i], x_recv.at[t, x], area, i)

    def halve(i, block):
        units = block.astype(jnp.int32)
        high = (units + 128) >> 8
        halves[i, :ROWS] = high.astype(F32).astype(BF16)
        halves[i, ROWS:] = (units - (high << 8)).astype(F32).astype(BF16)

    def product(i, sources):
        both = jnp.dot(halves[i], sources, preferred_element_type=F32)
        return (both[:ROWS] * 256.0 + both[ROWS:]) * (1.0 / UNITS)

    targets = [(ss, cc) for ss in far for cc in (c, 1 - c)] + [(s, 1 - c)]

    for pp in near:
        table_copy(pp).start()
    for i in across:
        w_copy(i).start()
    for pp in near:
        first_copy(pp).start()

    for pp in every:
        if pp is not every[0]:
            arrive(tables.at[pp], table_recv.at[pp])
        row = tables[pp, pl.ds(p, 1), :]
        wanted = jnp.concatenate(
            [jnp.broadcast_to(row[:, h * ROWS : (h + 1) * ROWS], (ROWS, ROWS)).T for h in range(2)], axis=0
        )[:CODES]
        lane = lax.broadcasted_iota(jnp.int32, (CODES, ROWS), 1).astype(F32)
        for b in range(DEPTH):
            pick[pp, :, b * ROWS : (b + 1) * ROWS] = jnp.where(wanted == lane + float(b * ROWS), 1.0, 0.0).astype(BF16)

    halve(x, w[x])

    def step(t, is_first):
        for pp in near:
            if is_first:
                arrive(held.at[pp, pl.ds(0, DEPTH)], first_recv.at[pp])
            else:
                arrive(held.at[pp, t + DEPTH - 1], hop1_recv.at[t, pp])
        for src in range(SIDE):
            states = jnp.concatenate([held[src, t + DEPTH - 1 - b] for b in range(DEPTH)], axis=0)
            mixed[pl.ds(src, CODES, stride=SIDE), :] = jnp.dot(pick[src], states, preferred_element_type=F32)
        for a in range(2 * SIDE):
            msg[t, a] = mixed[a * MSG : (a + 1) * MSG, :].astype(BF16)
        for ss, cc in targets:
            hop2_copy(t, ss, cc).start()
        got[t, c * SIDE + s] = msg[t, s * 2 + c]
        if is_first:
            for i in across:
                arrive(wg.at[i], w_recv.at[i])
                halve(i, wg[i])
        for ss in far:
            arrive(got.at[t, c * SIDE + ss], hop2_recv.at[t, c * SIDE + ss])
        for pp in every:
            arrive(got.at[t, (1 - c) * SIDE + pp], hop2_recv.at[t, (1 - c) * SIDE + pp])
        sources = jnp.concatenate([got[t].reshape(LONG, ROWS), held[p, t + DEPTH - 1]], axis=0)
        for i in across:
            part[t, i] = product(i, sources).astype(BF16)
            x_copy(t, i).start()
        total = product(x, sources) + drive[...]
        for i in across:
            arrive(parts.at[t, i], x_recv.at[t, i])
            total += parts[t, i].astype(F32)
        old = rate[...]
        new = mask[...] * (old + pace[...] * (jnp.tanh(total) - old))
        return new

    def advance(t, is_first):
        new = step(t, is_first)
        rate[...] = new
        held[p, t + DEPTH] = new.astype(BF16)
        for pp in near:
            hop1_copy(t + 1, pp).start()
        for ss, cc in targets:
            hop2_copy(t, ss, cc).wait_send()
        for i in across:
            x_copy(t, i).wait_send()
        if is_first:
            for pp in near:
                table_copy(pp).wait_send()
                first_copy(pp).wait_send()
            for i in across:
                w_copy(i).wait_send()
        else:
            for pp in near:
                hop1_copy(t, pp).wait_send()

    advance(0, True)

    @pl.loop(1, STEPS - 1)
    def _(t):
        advance(t, False)

    last = STEPS - 1
    out[...] = step(last, False)
    for pp in near:
        hop1_copy(last, pp).wait_send()
    for ss, cc in targets:
        hop2_copy(last, ss, cc).wait_send()
    for i in across:
        x_copy(last, i).wait_send()


def place_of_columns():
    place = np.zeros((2 * SIDE * SIDE * PROJ,), np.int32)
    for zz in range(SIDE):
        for yy in range(SIDE):
            for cc in range(2):
                for q in range(PROJ):
                    mid, src = (yy, zz) if cc == 0 else (SIDE + zz, yy)
                    place[((zz * SIDE + yy) * 2 + cc) * PROJ + q] = mid * MSG + q * SIDE + src
    return place


def local(history, drive, leak, w_local, w_long, sender_rows, delays, area_sizes):
    c = lax.axis_index("area") % 2
    picked = (delays[0] - 1)[:, None] * ROWS + sender_rows[0]
    by_z = picked.reshape(SIDE, 2 * SIDE, PROJ)
    by_y = picked.reshape(SIDE, SIDE, 2, PROJ).transpose(1, 0, 2, 3).reshape(SIDE, 2 * SIDE, PROJ)
    table = jnp.where(c == 0, by_z, by_y)
    table = jnp.pad(table, ((0, 0), (0, 0), (0, SLOTS - PROJ)), constant_values=-1).reshape(SIDE, CODES)
    table = jnp.pad(table, ((0, 0), (0, 2 * ROWS - CODES)), constant_values=-1).astype(F32)

    place = jnp.asarray(place_of_columns())
    spread = (place[:, None] == jnp.arange(LONG, dtype=jnp.int32)[None, :]).astype(BF16)
    units = jnp.round(w_long * UNITS).astype(jnp.int32)
    high = (units + 128) >> 8
    low = units - (high << 8)
    move = lambda a: jnp.einsum("nkc,cd->knd", a.astype(BF16), spread, preferred_element_type=F32)
    long = (move(high) * 256.0 + move(low)).astype(jnp.int32)
    near = jnp.round(w_local * UNITS).astype(jnp.int32).reshape(ROWS, PEERS, ROWS).transpose(1, 0, 2)
    w = jnp.concatenate([long, near], axis=2).astype(jnp.int16)

    vmem = pl.BlockSpec(memory_space=pltpu.VMEM)
    dma = pltpu.SemaphoreType.DMA
    return pl.pallas_call(
        kernel,
        out_shape=jax.ShapeDtypeStruct((ROWS, ROWS), F32),
        in_specs=[vmem, vmem, vmem, pl.BlockSpec(memory_space=pltpu.SMEM), vmem, vmem],
        out_specs=vmem,
        scratch_shapes=[
            pltpu.VMEM((SIDE, SIDE, 2 * ROWS), F32),
            pltpu.VMEM((SIDE, DEPTH + STEPS, ROWS, ROWS), BF16),
            pltpu.VMEM((SIDE, CODES, DEPTH * ROWS), BF16),
            pltpu.VMEM((LONG, ROWS), F32),
            pltpu.VMEM((STEPS, 2 * SIDE, MSG, ROWS), BF16),
            pltpu.VMEM((STEPS, 2 * SIDE, MSG, ROWS), BF16),
            pltpu.VMEM((PEERS, ROWS, LONG + ROWS), jnp.int16),
            pltpu.VMEM((PEERS, 2 * ROWS, LONG + ROWS), BF16),
            pltpu.VMEM((STEPS, PEERS, ROWS, ROWS), BF16),
            pltpu.VMEM((STEPS, PEERS, ROWS, ROWS), BF16),
            pltpu.VMEM((ROWS, ROWS), F32),
            pltpu.VMEM((ROWS, ROWS), F32),
            pltpu.VMEM((ROWS, ROWS), F32),
            dma((SIDE,)), dma((SIDE,)), dma((SIDE,)), dma((SIDE,)), dma((PEERS,)), dma((PEERS,)),
            dma((STEPS, SIDE)), dma((STEPS, SIDE)), dma((STEPS, 2 * SIDE)), dma((STEPS, 2 * SIDE)),
            dma((STEPS, PEERS)), dma((STEPS, PEERS)),
        ],
        compiler_params=pltpu.CompilerParams(
            collective_id=0, has_side_effects=True, vmem_limit_bytes=48 * 1024 * 1024
        ),
        cost_estimate=pl.CostEstimate(flops=2 * 10**9, bytes_accessed=4 * 10**6, transcendentals=10**5),
    )(history, drive, leak.reshape(1, ROWS), area_sizes, table, w)


def solution(mesh):
    placed = (
        P(None, ("area", "nrn"), None),
        P(("area", "nrn"), None),
        P(("area", "nrn")),
        P(("area", "nrn"), None),
        P(("area", "nrn"), None, None),
        P(("area", "nrn"), None, None),
        P("area", None),
        P("area"),
    )
    return jax.shard_map(
        local, mesh=mesh, in_specs=placed, out_specs=P(("area", "nrn"), None), check_vma=False
    )
```

```python
import jax
import jax.numpy as jnp
import numpy as np
from jax import lax
from jax.experimental import pallas as pl
from jax.experimental.pallas import tpu as pltpu
from jax.sharding import PartitionSpec as P

STEPS = 6
SIDE = 8
PEERS = 4
DEPTH = 4
ROWS = 128
PROJ = 9
SLOTS = 10
MSG = SLOTS * SIDE
CODES = 2 * SIDE * PROJ
LONG = 2 * SIDE * MSG
COLUMNS = 2 * SIDE * SIDE * PROJ
ORDER = (4, 3, 5, 2, 6, 1, 7)
MESH = pl.DeviceIdType.MESH
F32 = jnp.float32
BF16 = jnp.bfloat16
UNITS = 32767.0 / 0.25


def kernel(
    history, drive, leak, sizes, sender_rows, delays, w_local, w_long, spread, out,
    codes, table, tables, held, pick, mixed, msg, got, early, early_in, raw, moves, rows_in, w, wg, halves, part, parts, rate, mask, pace,
    load_sem, early_send, early_recv,
    table_send, table_recv, first_send, first_recv, w_send, w_recv,
    hop1_send, hop1_recv, hop2_send, hop2_recv, x_send, x_recv,
):
    area = lax.axis_index("area")
    x = lax.axis_index("nrn")
    c = area % 2
    y = (area // 2) % SIDE
    z = area // (2 * SIDE)
    p = z + (y - z) * c
    s = y + (z - y) * c
    p_stride = 2 * SIDE + (2 - 2 * SIDE) * c
    s_stride = 2 + (2 * SIDE - 2) * c

    def at(pp, ss, cc):
        return pp * p_stride + ss * s_stride + cc

    def remote(src, dst, send, recv, target_area, target_x):
        return pltpu.make_async_remote_copy(
            src_ref=src, dst_ref=dst, send_sem=send, recv_sem=recv,
            device_id=(target_area, target_x), device_id_type=MESH,
        )

    def arrive(ref, recv):
        remote(ref, ref, recv, recv, area, x).wait_recv()

    near = [(p + r) % SIDE for r in ORDER]
    far = [(s + r) % SIDE for r in ORDER]
    every = [(p + r) % SIDE for r in (0,) + ORDER]
    across = [(x + r) % PEERS for r in (2, 1, 3)]

    loads = [pltpu.make_async_copy(w_long, raw, load_sem.at[0]), pltpu.make_async_copy(spread, moves, load_sem.at[1]),
             pltpu.make_async_copy(sender_rows, rows_in, load_sem.at[2])]
    for load in loads:
        load.start()

    barrier = pltpu.get_barrier_semaphore()
    for pp in near:
        pl.semaphore_signal(barrier, inc=1, device_id=(at(pp, s, c), x), device_id_type=MESH)
    for ss in far:
        pl.semaphore_signal(barrier, inc=1, device_id=(at(p, ss, c), x), device_id_type=MESH)
    for pp in every:
        pl.semaphore_signal(barrier, inc=1, device_id=(at(pp, s, 1 - c), x), device_id_type=MESH)
    for i in across:
        pl.semaphore_signal(barrier, inc=1, device_id=(area, i), device_id_type=MESH)

    alive = (lax.broadcasted_iota(jnp.int32, (ROWS, ROWS), 0) + x * ROWS < sizes[0]).astype(F32)
    mask[...] = alive
    pace[...] = jnp.broadcast_to(leak[...], (ROWS, ROWS)).T
    rate[...] = history[0] * alive
    for i in range(DEPTH):
        held[p, DEPTH - 1 - i] = (history[i] * alive).astype(BF16)

    loads[2].wait()
    lags = jnp.broadcast_to(delays[...].astype(F32), (ROWS, ROWS)).T
    codes[...] = jnp.full((ROWS, ROWS), -1.0, F32)
    codes[:, :PROJ] = (lags[:, :PROJ] - 1.0) * ROWS + rows_in[0].astype(F32)
    for pp in range(SIDE):
        for ss in range(SIDE):
            table[pp, 2 * ss : 2 * ss + 2, :] = codes[pl.ds(at(pp, ss, 0), 2), :]
    tables[p] = table[p]
    mixed[...] = jnp.zeros(mixed.shape, F32)

    def table_copy(pp):
        return remote(table.at[pp], tables.at[p], table_send.at[pp], table_recv.at[p], at(pp, s, c), x)

    def first_copy(pp):
        ref = held.at[p, pl.ds(1, DEPTH - 1)]
        return remote(ref, ref, first_send.at[pp], first_recv.at[p], at(pp, s, c), x)

    def w_copy(i):
        return remote(w.at[i], wg.at[x], w_send.at[i], w_recv.at[x], area, i)

    def hop1_copy(t, pp):
        ref = held.at[p, t + DEPTH - 1]
        return remote(ref, ref, hop1_send.at[t, pp], hop1_recv.at[t, p], at(pp, s, c), x)

    def hop2_copy(t, ss, cc):
        a = ss * 2 + cc
        return remote(
            msg.at[t, a], got.at[t, c * SIDE + s], hop2_send.at[t, a], hop2_recv.at[t, c * SIDE + s], at(p, ss, cc), x
        )

    def x_copy(t, i):
        return remote(part.at[t, i], parts.at[t, x], x_send.at[t, i], x_recv.at[t, x], area, i)

    def halve(i, block):
        units = block.astype(jnp.int32)
        high = (units + 128) >> 8
        halves[i, :ROWS] = high.astype(F32).astype(BF16)
        halves[i, ROWS:] = (units - (high << 8)).astype(F32).astype(BF16)

    def product(i, sources):
        both = jnp.dot(halves[i], sources, preferred_element_type=F32)
        return (both[:ROWS] * 256.0 + both[ROWS:]) * (1.0 / UNITS)

    targets = [(ss, cc) for ss in far for cc in (c, 1 - c)] + [(s, 1 - c)]

    def early_copy(pp):
        return remote(early.at[pp], early_in.at[p], early_send.at[pp], early_recv.at[p], at(pp, s, c), x)

    lane = lax.broadcasted_iota(jnp.int32, (2 * SIDE, ROWS), 1).astype(F32)

    def one_hot(wanted, index):
        for q in range(PROJ):
            column = jnp.broadcast_to(wanted[:, q : q + 1], (2 * SIDE, ROWS))
            for b in range(DEPTH):
                pick[index, q * 2 * SIDE : (q + 1) * 2 * SIDE, b * ROWS : (b + 1) * ROWS] = jnp.where(
                    column == lane + float(b * ROWS), 1.0, 0.0
                ).astype(BF16)

    states = jnp.concatenate([held[p, DEPTH - 1 - b] for b in range(DEPTH)], axis=0)
    for pp in range(SIDE):
        one_hot(table[pp], pp)
        early[pp] = jnp.dot(pick[pp], states, preferred_element_type=F32).astype(BF16)

    loads[0].wait()
    loads[1].wait()
    def prepare(k):
        units = jnp.round(raw[:, k, :] * UNITS).astype(jnp.int32)
        high = (units + 128) >> 8
        both = jnp.concatenate([high, units - (high << 8)], axis=0).astype(F32).astype(BF16)
        moved = jnp.dot(both, moves[...], preferred_element_type=F32)
        w[k, :, :LONG] = (moved[:ROWS] * 256.0 + moved[ROWS:]).astype(jnp.int32).astype(jnp.int16)
        near_units = jnp.round(w_local[:, k * ROWS : (k + 1) * ROWS] * UNITS)
        w[k, :, LONG:] = near_units.astype(jnp.int32).astype(jnp.int16)

    def give(k):
        @pl.when(k != x)
        def _():
            w_copy(k).start()

    for k in range(PEERS // 2):
        prepare(k)

    pl.semaphore_wait(barrier, 2 * len(near) + len(every) + len(across))

    for pp in near:
        early_copy(pp).start()
    for k in range(PEERS):
        if k >= PEERS // 2:
            prepare(k)
        give(k)
    for pp in near:
        table_copy(pp).start()

    def step(t, is_first, is_second=False):
        for pp in every:
            if is_first:
                if pp is not every[0]:
                    arrive(early_in.at[pp], early_recv.at[pp])
                    rows = early_in[pp].astype(F32)
                else:
                    rows = early[p].astype(F32)
            else:
                if pp is not every[0]:
                    if is_second:
                        arrive(held.at[pp, pl.ds(1, DEPTH - 1)], first_recv.at[pp])
                    arrive(held.at[pp, t + DEPTH - 1], hop1_recv.at[t, pp])
                states = jnp.concatenate([held[pp, t + DEPTH - 1 - b] for b in range(DEPTH)], axis=0)
                rows = jnp.dot(pick[pp], states, preferred_element_type=F32)
            for q in range(PROJ):
                mixed[pl.ds(q * SIDE + pp, 2 * SIDE, stride=MSG), :] = rows[q * 2 * SIDE : (q + 1) * 2 * SIDE]
        for a in range(2 * SIDE):
            msg[t, a] = mixed[a * MSG : (a + 1) * MSG, :].astype(BF16)
        for ss, cc in targets:
            hop2_copy(t, ss, cc).start()
        got[t, c * SIDE + s] = msg[t, s * 2 + c]
        if is_first:
            for pp in near:
                first_copy(pp).start()
            for pp in every:
                if pp is not every[0]:
                    arrive(tables.at[pp], table_recv.at[pp])
                one_hot(tables[pp], pp)
            halve(x, w[x])
            for i in across:
                arrive(wg.at[i], w_recv.at[i])
                halve(i, wg[i])
        for ss in far:
            arrive(got.at[t, c * SIDE + ss], hop2_recv.at[t, c * SIDE + ss])
        for pp in every:
            arrive(got.at[t, (1 - c) * SIDE + pp], hop2_recv.at[t, (1 - c) * SIDE + pp])
        sources = jnp.concatenate([got[t].reshape(LONG, ROWS), held[p, t + DEPTH - 1]], axis=0)
        for i in across:
            part[t, i] = product(i, sources).astype(BF16)
            x_copy(t, i).start()
        total = product(x, sources) + drive[...]
        for i in across:
            arrive(parts.at[t, i], x_recv.at[t, i])
            total += parts[t, i].astype(F32)
        old = rate[...]
        new = mask[...] * (old + pace[...] * (jnp.tanh(total) - old))
        return new

    def advance(t, is_first, is_second=False):
        new = step(t, is_first, is_second)
        rate[...] = new
        held[p, t + DEPTH] = new.astype(BF16)
        for pp in near:
            hop1_copy(t + 1, pp).start()
        for ss, cc in targets:
            hop2_copy(t, ss, cc).wait_send()
        for i in across:
            x_copy(t, i).wait_send()
        if is_first:
            for pp in near:
                table_copy(pp).wait_send()
                early_copy(pp).wait_send()
            for i in across:
                w_copy(i).wait_send()
        else:
            for pp in near:
                if is_second:
                    first_copy(pp).wait_send()
                hop1_copy(t, pp).wait_send()

    advance(0, True)
    advance(1, False, True)

    @pl.loop(2, STEPS - 1)
    def _(t):
        advance(t, False)

    last = STEPS - 1
    out[...] = step(last, False)
    for pp in near:
        hop1_copy(last, pp).wait_send()
    for ss, cc in targets:
        hop2_copy(last, ss, cc).wait_send()
    for i in across:
        x_copy(last, i).wait_send()


def place_of_columns():
    place = np.zeros((2 * SIDE * SIDE * PROJ,), np.int32)
    for zz in range(SIDE):
        for yy in range(SIDE):
            for cc in range(2):
                for q in range(PROJ):
                    mid, src = (yy, zz) if cc == 0 else (SIDE + zz, yy)
                    place[((zz * SIDE + yy) * 2 + cc) * PROJ + q] = mid * MSG + q * SIDE + src
    return place


def local(history, drive, leak, w_local, w_long, sender_rows, delays, area_sizes):
    spread = jnp.asarray(place_of_columns()[:, None] == np.arange(LONG)[None, :], BF16)
    vmem = pl.BlockSpec(memory_space=pltpu.VMEM)
    hbm = pl.BlockSpec(memory_space=pl.ANY)
    dma = pltpu.SemaphoreType.DMA
    return pl.pallas_call(
        kernel,
        out_shape=jax.ShapeDtypeStruct((ROWS, ROWS), F32),
        in_specs=[vmem, vmem, vmem, pl.BlockSpec(memory_space=pltpu.SMEM), hbm, vmem, vmem, hbm, hbm],
        out_specs=vmem,
        scratch_shapes=[
            pltpu.VMEM((ROWS, ROWS), F32),
            pltpu.VMEM((SIDE, 2 * SIDE, ROWS), F32),
            pltpu.VMEM((SIDE, 2 * SIDE, ROWS), F32),
            pltpu.VMEM((SIDE, DEPTH + STEPS, ROWS, ROWS), BF16),
            pltpu.VMEM((SIDE, CODES, DEPTH * ROWS), BF16),
            pltpu.VMEM((LONG, ROWS), F32),
            pltpu.VMEM((STEPS, 2 * SIDE, MSG, ROWS), BF16),
            pltpu.VMEM((STEPS, 2 * SIDE, MSG, ROWS), BF16),
            pltpu.VMEM((SIDE, CODES, ROWS), BF16),
            pltpu.VMEM((SIDE, CODES, ROWS), BF16),
            pltpu.VMEM((ROWS, PEERS, COLUMNS), F32),
            pltpu.VMEM((COLUMNS, LONG), BF16),
            pltpu.VMEM((1, ROWS, PROJ), jnp.int32),
            pltpu.VMEM((PEERS, ROWS, LONG + ROWS), jnp.int16),
            pltpu.VMEM((PEERS, ROWS, LONG + ROWS), jnp.int16),
            pltpu.VMEM((PEERS, 2 * ROWS, LONG + ROWS), BF16),
            pltpu.VMEM((STEPS, PEERS, ROWS, ROWS), BF16),
            pltpu.VMEM((STEPS, PEERS, ROWS, ROWS), BF16),
            pltpu.VMEM((ROWS, ROWS), F32),
            pltpu.VMEM((ROWS, ROWS), F32),
            pltpu.VMEM((ROWS, ROWS), F32),
            dma((3,)), dma((SIDE,)), dma((SIDE,)), dma((SIDE,)), dma((SIDE,)), dma((SIDE,)), dma((SIDE,)), dma((PEERS,)), dma((PEERS,)),
            dma((STEPS, SIDE)), dma((STEPS, SIDE)), dma((STEPS, 2 * SIDE)), dma((STEPS, 2 * SIDE)),
            dma((STEPS, PEERS)), dma((STEPS, PEERS)),
        ],
        compiler_params=pltpu.CompilerParams(
            collective_id=0, has_side_effects=True, vmem_limit_bytes=60 * 1024 * 1024
        ),
        cost_estimate=pl.CostEstimate(flops=2 * 10**9, bytes_accessed=4 * 10**6, transcendentals=10**5),
    )(history, drive, leak.reshape(1, ROWS), area_sizes, sender_rows, delays, w_local, w_long, spread)


def solution(mesh):
    placed = (
        P(None, ("area", "nrn"), None),
        P(("area", "nrn"), None),
        P(("area", "nrn")),
        P(("area", "nrn"), None),
        P(("area", "nrn"), None, None),
        P(("area", "nrn"), None, None),
        P("area", None),
        P("area"),
    )
    return jax.shard_map(
        local, mesh=mesh, in_specs=placed, out_specs=P(("area", "nrn"), None), check_vma=False
    )
```

```python
import jax
import jax.numpy as jnp
import numpy as np
from jax import lax
from jax.experimental import pallas as pl
from jax.experimental.pallas import tpu as pltpu
from jax.sharding import PartitionSpec as P

STEPS = 6
SIDE = 8
PEERS = 4
DEPTH = 4
ROWS = 128
PROJ = 9
SLOTS = 10
MSG = SLOTS * SIDE
CODES = 2 * SIDE * PROJ
LONG = 2 * SIDE * MSG
COLUMNS = 2 * SIDE * SIDE * PROJ
ORDER = (4, 3, 5, 2, 6, 1, 7)
MESH = pl.DeviceIdType.MESH
F32 = jnp.float32
BF16 = jnp.bfloat16
UNITS = 32767.0 / 0.25


def kernel(
    history, drive, leak, sizes, sender_rows, delays, w_local, w_long, spread, out,
    codes, table, tables, held, pick, mixed, msg, got, early, early_in, raw, moves, rows_in, w, wg, halves, part, parts, rate, mask, pace,
    load_sem, early_send, early_recv,
    table_send, table_recv, first_send, first_recv, w_send, w_recv,
    hop1_send, hop1_recv, hop2_send, hop2_recv, x_send, x_recv,
):
    area = lax.axis_index("area")
    x = lax.axis_index("nrn")
    c = area % 2
    y = (area // 2) % SIDE
    z = area // (2 * SIDE)
    p = z + (y - z) * c
    s = y + (z - y) * c
    p_stride = 2 * SIDE + (2 - 2 * SIDE) * c
    s_stride = 2 + (2 * SIDE - 2) * c

    def at(pp, ss, cc):
        return pp * p_stride + ss * s_stride + cc

    def remote(src, dst, send, recv, target_area, target_x):
        return pltpu.make_async_remote_copy(
            src_ref=src, dst_ref=dst, send_sem=send, recv_sem=recv,
            device_id=(target_area, target_x), device_id_type=MESH,
        )

    def arrive(ref, recv):
        remote(ref, ref, recv, recv, area, x).wait_recv()

    near = [(p + r) % SIDE for r in ORDER]
    far = [(s + r) % SIDE for r in ORDER]
    every = [(p + r) % SIDE for r in (0,) + ORDER]
    across = [(x + r) % PEERS for r in (2, 1, 3)]

    loads = [pltpu.make_async_copy(w_long, raw, load_sem.at[0]), pltpu.make_async_copy(spread, moves, load_sem.at[1]),
             pltpu.make_async_copy(sender_rows, rows_in, load_sem.at[2])]
    for load in loads:
        load.start()

    barrier = pltpu.get_barrier_semaphore()
    for pp in near:
        pl.semaphore_signal(barrier, inc=1, device_id=(at(pp, s, c), x), device_id_type=MESH)
    for ss in far:
        pl.semaphore_signal(barrier, inc=1, device_id=(at(p, ss, c), x), device_id_type=MESH)
    for pp in every:
        pl.semaphore_signal(barrier, inc=1, device_id=(at(pp, s, 1 - c), x), device_id_type=MESH)
    for i in across:
        pl.semaphore_signal(barrier, inc=1, device_id=(area, i), device_id_type=MESH)

    alive = (lax.broadcasted_iota(jnp.int32, (ROWS, ROWS), 0) + x * ROWS < sizes[0]).astype(F32)
    mask[...] = alive
    pace[...] = jnp.broadcast_to(leak[...], (ROWS, ROWS)).T
    rate[...] = history[0] * alive
    for i in range(DEPTH):
        held[p, DEPTH - 1 - i] = (history[i] * alive).astype(BF16)

    loads[2].wait()
    codes[...] = jnp.full((ROWS, ROWS), -1.0, F32)
    for q in range(PROJ):
        codes[q : q + 1, :] = (delays[...].astype(F32) - 1.0) * ROWS + rows_in[q].astype(F32)
    codes[...] = codes[...].T
    for pp in range(SIDE):
        for ss in range(SIDE):
            table[pp, 2 * ss : 2 * ss + 2, :] = codes[pl.ds(at(pp, ss, 0), 2), :]
    tables[p] = table[p]
    mixed[...] = jnp.zeros(mixed.shape, F32)

    def table_copy(pp):
        return remote(table.at[pp], tables.at[p], table_send.at[pp], table_recv.at[p], at(pp, s, c), x)

    def first_copy(pp):
        ref = held.at[p, pl.ds(1, DEPTH - 1)]
        return remote(ref, ref, first_send.at[pp], first_recv.at[p], at(pp, s, c), x)

    def w_copy(i):
        return remote(w.at[i], wg.at[x], w_send.at[i], w_recv.at[x], area, i)

    def hop1_copy(t, pp):
        ref = held.at[p, t + DEPTH - 1]
        return remote(ref, ref, hop1_send.at[t, pp], hop1_recv.at[t, p], at(pp, s, c), x)

    def hop2_copy(t, ss, cc):
        a = ss * 2 + cc
        return remote(
            msg.at[t, a], got.at[t, c * SIDE + s], hop2_send.at[t, a], hop2_recv.at[t, c * SIDE + s], at(p, ss, cc), x
        )

    def x_copy(t, i):
        return remote(part.at[t, i], parts.at[t, x], x_send.at[t, i], x_recv.at[t, x], area, i)

    def halve(i, block):
        units = block.astype(jnp.int32)
        high = (units + 128) >> 8
        halves[i, :ROWS] = high.astype(F32).astype(BF16)
        halves[i, ROWS:] = (units - (high << 8)).astype(F32).astype(BF16)

    def product(i, sources):
        both = jnp.dot(halves[i], sources, preferred_element_type=F32)
        return (both[:ROWS] * 256.0 + both[ROWS:]) * (1.0 / UNITS)

    targets = [(ss, cc) for ss in far for cc in (c, 1 - c)] + [(s, 1 - c)]

    def early_copy(pp):
        return remote(early.at[pp], early_in.at[p], early_send.at[pp], early_recv.at[p], at(pp, s, c), x)

    lane = lax.broadcasted_iota(jnp.int32, (2 * SIDE, ROWS), 1).astype(F32)

    def one_hot(wanted, index):
        for q in range(PROJ):
            column = jnp.broadcast_to(wanted[:, q : q + 1], (2 * SIDE, ROWS))
            for b in range(DEPTH):
                pick[index, q * 2 * SIDE : (q + 1) * 2 * SIDE, b * ROWS : (b + 1) * ROWS] = jnp.where(
                    column == lane + float(b * ROWS), 1.0, 0.0
                ).astype(BF16)

    states = jnp.concatenate([held[p, DEPTH - 1 - b] for b in range(DEPTH)], axis=0)
    for pp in range(SIDE):
        one_hot(table[pp], pp)
        early[pp] = jnp.dot(pick[pp], states, preferred_element_type=F32).astype(BF16)

    loads[0].wait()
    loads[1].wait()
    def prepare(k):
        units = jnp.round(raw[:, k, :] * UNITS).astype(jnp.int32)
        high = (units + 128) >> 8
        both = jnp.concatenate([high, units - (high << 8)], axis=0).astype(F32).astype(BF16)
        moved = jnp.dot(both, moves[...], preferred_element_type=F32)
        w[k, :, :LONG] = (moved[:ROWS] * 256.0 + moved[ROWS:]).astype(jnp.int32).astype(jnp.int16)
        near_units = jnp.round(w_local[:, k * ROWS : (k + 1) * ROWS] * UNITS)
        w[k, :, LONG:] = near_units.astype(jnp.int32).astype(jnp.int16)

    def give(k):
        @pl.when(k != x)
        def _():
            w_copy(k).start()

    for k in range(PEERS // 2):
        prepare(k)

    pl.semaphore_wait(barrier, 2 * len(near) + len(every) + len(across))

    for pp in near:
        early_copy(pp).start()
    for k in range(PEERS):
        if k >= PEERS // 2:
            prepare(k)
        give(k)
    for pp in near:
        table_copy(pp).start()

    def step(t, is_first, is_second=False):
        for pp in every:
            if is_first:
                if pp is not every[0]:
                    arrive(early_in.at[pp], early_recv.at[pp])
                    rows = early_in[pp].astype(F32)
                else:
                    rows = early[p].astype(F32)
            else:
                if pp is not every[0]:
                    if is_second:
                        arrive(held.at[pp, pl.ds(1, DEPTH - 1)], first_recv.at[pp])
                    arrive(held.at[pp, t + DEPTH - 1], hop1_recv.at[t, pp])
                states = jnp.concatenate([held[pp, t + DEPTH - 1 - b] for b in range(DEPTH)], axis=0)
                rows = jnp.dot(pick[pp], states, preferred_element_type=F32)
            for q in range(PROJ):
                mixed[pl.ds(q * SIDE + pp, 2 * SIDE, stride=MSG), :] = rows[q * 2 * SIDE : (q + 1) * 2 * SIDE]
        for a in range(2 * SIDE):
            msg[t, a] = mixed[a * MSG : (a + 1) * MSG, :].astype(BF16)
        for ss, cc in targets:
            hop2_copy(t, ss, cc).start()
        got[t, c * SIDE + s] = msg[t, s * 2 + c]
        if is_first:
            for pp in near:
                first_copy(pp).start()
            for pp in every:
                if pp is not every[0]:
                    arrive(tables.at[pp], table_recv.at[pp])
                one_hot(tables[pp], pp)
            halve(x, w[x])
        for ss in far:
            arrive(got.at[t, c * SIDE + ss], hop2_recv.at[t, c * SIDE + ss])
        for pp in every:
            arrive(got.at[t, (1 - c) * SIDE + pp], hop2_recv.at[t, (1 - c) * SIDE + pp])
        sources = jnp.concatenate([got[t].reshape(LONG, ROWS), held[p, t + DEPTH - 1]], axis=0)
        for i in across[1:] + across[:1] if is_first else across:
            if is_first:
                arrive(wg.at[i], w_recv.at[i])
                halve(i, wg[i])
            part[t, i] = product(i, sources).astype(BF16)
            x_copy(t, i).start()
        total = product(x, sources) + drive[...]
        for i in across:
            arrive(parts.at[t, i], x_recv.at[t, i])
            total += parts[t, i].astype(F32)
        old = rate[...]
        new = mask[...] * (old + pace[...] * (jnp.tanh(total) - old))
        return new

    def advance(t, is_first, is_second=False):
        new = step(t, is_first, is_second)
        rate[...] = new
        held[p, t + DEPTH] = new.astype(BF16)
        for pp in near:
            hop1_copy(t + 1, pp).start()
        for ss, cc in targets:
            hop2_copy(t, ss, cc).wait_send()
        for i in across:
            x_copy(t, i).wait_send()
        if is_first:
            for pp in near:
                table_copy(pp).wait_send()
                early_copy(pp).wait_send()
            for i in across:
                w_copy(i).wait_send()
        else:
            for pp in near:
                if is_second:
                    first_copy(pp).wait_send()
                hop1_copy(t, pp).wait_send()

    advance(0, True)
    advance(1, False, True)

    @pl.loop(2, STEPS - 1)
    def _(t):
        advance(t, False)

    last = STEPS - 1
    out[...] = step(last, False)
    for pp in near:
        hop1_copy(last, pp).wait_send()
    for ss, cc in targets:
        hop2_copy(last, ss, cc).wait_send()
    for i in across:
        x_copy(last, i).wait_send()


def place_of_columns():
    place = np.zeros((2 * SIDE * SIDE * PROJ,), np.int32)
    for zz in range(SIDE):
        for yy in range(SIDE):
            for cc in range(2):
                for q in range(PROJ):
                    mid, src = (yy, zz) if cc == 0 else (SIDE + zz, yy)
                    place[((zz * SIDE + yy) * 2 + cc) * PROJ + q] = mid * MSG + q * SIDE + src
    return place


def local(history, drive, leak, w_local, w_long, sender_rows, delays, area_sizes):
    spread = jnp.asarray(place_of_columns()[:, None] == np.arange(LONG)[None, :], BF16)
    vmem = pl.BlockSpec(memory_space=pltpu.VMEM)
    hbm = pl.BlockSpec(memory_space=pl.ANY)
    dma = pltpu.SemaphoreType.DMA
    return pl.pallas_call(
        kernel,
        out_shape=jax.ShapeDtypeStruct((ROWS, ROWS), F32),
        in_specs=[vmem, vmem, vmem, pl.BlockSpec(memory_space=pltpu.SMEM), hbm, vmem, vmem, hbm, hbm],
        out_specs=vmem,
        scratch_shapes=[
            pltpu.VMEM((ROWS, ROWS), F32),
            pltpu.VMEM((SIDE, 2 * SIDE, ROWS), F32),
            pltpu.VMEM((SIDE, 2 * SIDE, ROWS), F32),
            pltpu.VMEM((SIDE, DEPTH + STEPS, ROWS, ROWS), BF16),
            pltpu.VMEM((SIDE, CODES, DEPTH * ROWS), BF16),
            pltpu.VMEM((LONG, ROWS), F32),
            pltpu.VMEM((STEPS, 2 * SIDE, MSG, ROWS), BF16),
            pltpu.VMEM((STEPS, 2 * SIDE, MSG, ROWS), BF16),
            pltpu.VMEM((SIDE, CODES, ROWS), BF16),
            pltpu.VMEM((SIDE, CODES, ROWS), BF16),
            pltpu.VMEM((ROWS, PEERS, COLUMNS), F32),
            pltpu.VMEM((COLUMNS, LONG), BF16),
            pltpu.VMEM((PROJ, 1, ROWS), jnp.int32),
            pltpu.VMEM((PEERS, ROWS, LONG + ROWS), jnp.int16),
            pltpu.VMEM((PEERS, ROWS, LONG + ROWS), jnp.int16),
            pltpu.VMEM((PEERS, 2 * ROWS, LONG + ROWS), BF16),
            pltpu.VMEM((STEPS, PEERS, ROWS, ROWS), BF16),
            pltpu.VMEM((STEPS, PEERS, ROWS, ROWS), BF16),
            pltpu.VMEM((ROWS, ROWS), F32),
            pltpu.VMEM((ROWS, ROWS), F32),
            pltpu.VMEM((ROWS, ROWS), F32),
            dma((3,)), dma((SIDE,)), dma((SIDE,)), dma((SIDE,)), dma((SIDE,)), dma((SIDE,)), dma((SIDE,)), dma((PEERS,)), dma((PEERS,)),
            dma((STEPS, SIDE)), dma((STEPS, SIDE)), dma((STEPS, 2 * SIDE)), dma((STEPS, 2 * SIDE)),
            dma((STEPS, PEERS)), dma((STEPS, PEERS)),
        ],
        compiler_params=pltpu.CompilerParams(
            collective_id=0, has_side_effects=True, vmem_limit_bytes=60 * 1024 * 1024
        ),
        cost_estimate=pl.CostEstimate(flops=2 * 10**9, bytes_accessed=4 * 10**6, transcendentals=10**5),
    )(history, drive, leak.reshape(1, ROWS), area_sizes, sender_rows.transpose(2, 0, 1), delays, w_local, w_long, spread)


def solution(mesh):
    placed = (
        P(None, ("area", "nrn"), None),
        P(("area", "nrn"), None),
        P(("area", "nrn")),
        P(("area", "nrn"), None),
        P(("area", "nrn"), None, None),
        P(("area", "nrn"), None, None),
        P("area", None),
        P("area"),
    )
    return jax.shard_map(
        local, mesh=mesh, in_specs=placed, out_specs=P(("area", "nrn"), None), check_vma=False
    )
```

```python
import jax
import jax.numpy as jnp
import numpy as np
from jax import lax
from jax.experimental import pallas as pl
from jax.experimental.pallas import tpu as pltpu
from jax.sharding import PartitionSpec as P

STEPS = 6
SIDE = 8
PEERS = 4
DEPTH = 4
ROWS = 128
PROJ = 9
SLOTS = 10
MSG = SLOTS * SIDE
CODES = 2 * SIDE * PROJ
LONG = 2 * SIDE * MSG
COLUMNS = 2 * SIDE * SIDE * PROJ
ORDER = (4, 3, 5, 2, 6, 1, 7)
MESH = pl.DeviceIdType.MESH
F32 = jnp.float32
BF16 = jnp.bfloat16
UNITS = 32767.0 / 0.25


def kernel(
    history, drive, leak, sizes, sender_rows, delays, w_local, w_long, spread, out,
    codes, table, tables, held, pick, older, mixed, msg, got, early, early_in, raw, moves, rows_in, w, wg, halves, part, parts, rate, mask, pace,
    load_sem, early_send, early_recv,
    table_send, table_recv, first_send, first_recv, w_send, w_recv,
    hop1_send, hop1_recv, hop2_send, hop2_recv, x_send, x_recv,
):
    area = lax.axis_index("area")
    x = lax.axis_index("nrn")
    c = area % 2
    y = (area // 2) % SIDE
    z = area // (2 * SIDE)
    p = z + (y - z) * c
    s = y + (z - y) * c
    p_stride = 2 * SIDE + (2 - 2 * SIDE) * c
    s_stride = 2 + (2 * SIDE - 2) * c

    def at(pp, ss, cc):
        return pp * p_stride + ss * s_stride + cc

    def remote(src, dst, send, recv, target_area, target_x):
        return pltpu.make_async_remote_copy(
            src_ref=src, dst_ref=dst, send_sem=send, recv_sem=recv,
            device_id=(target_area, target_x), device_id_type=MESH,
        )

    def arrive(ref, recv):
        remote(ref, ref, recv, recv, area, x).wait_recv()

    near = [(p + r) % SIDE for r in ORDER]
    far = [(s + r) % SIDE for r in ORDER]
    every = [(p + r) % SIDE for r in (0,) + ORDER]
    across = [(x + r) % PEERS for r in (2, 1, 3)]

    loads = [pltpu.make_async_copy(w_long, raw, load_sem.at[0]), pltpu.make_async_copy(spread, moves, load_sem.at[1]),
             pltpu.make_async_copy(sender_rows, rows_in, load_sem.at[2])]
    for load in loads:
        load.start()

    barrier = pltpu.get_barrier_semaphore()
    for pp in near:
        pl.semaphore_signal(barrier, inc=1, device_id=(at(pp, s, c), x), device_id_type=MESH)
    for ss in far:
        pl.semaphore_signal(barrier, inc=1, device_id=(at(p, ss, c), x), device_id_type=MESH)
    for pp in every:
        pl.semaphore_signal(barrier, inc=1, device_id=(at(pp, s, 1 - c), x), device_id_type=MESH)
    for i in across:
        pl.semaphore_signal(barrier, inc=1, device_id=(area, i), device_id_type=MESH)

    alive = (lax.broadcasted_iota(jnp.int32, (ROWS, ROWS), 0) + x * ROWS < sizes[0]).astype(F32)
    mask[...] = alive
    pace[...] = jnp.broadcast_to(leak[...], (ROWS, ROWS)).T
    rate[...] = history[0] * alive
    for i in range(DEPTH):
        held[p, DEPTH - 1 - i] = (history[i] * alive).astype(BF16)

    loads[2].wait()
    codes[...] = jnp.full((ROWS, ROWS), -1.0, F32)
    for q in range(PROJ):
        codes[q : q + 1, :] = (delays[...].astype(F32) - 1.0) * ROWS + rows_in[q].astype(F32)
    codes[...] = codes[...].T
    for pp in range(SIDE):
        for ss in range(SIDE):
            table[pp, 2 * ss : 2 * ss + 2, :] = codes[pl.ds(at(pp, ss, 0), 2), :]
    tables[p] = table[p]
    mixed[...] = jnp.zeros(mixed.shape, F32)

    def table_copy(pp):
        return remote(table.at[pp], tables.at[p], table_send.at[pp], table_recv.at[p], at(pp, s, c), x)

    def first_copy(pp):
        ref = held.at[p, pl.ds(1, DEPTH - 1)]
        return remote(ref, ref, first_send.at[pp], first_recv.at[p], at(pp, s, c), x)

    def w_copy(i):
        return remote(w.at[i], wg.at[x], w_send.at[i], w_recv.at[x], area, i)

    def hop1_copy(t, pp):
        ref = held.at[p, t + DEPTH - 1]
        return remote(ref, ref, hop1_send.at[t, pp], hop1_recv.at[t, p], at(pp, s, c), x)

    def hop2_copy(t, ss, cc):
        a = ss * 2 + cc
        return remote(
            msg.at[t, a], got.at[t, c * SIDE + s], hop2_send.at[t, a], hop2_recv.at[t, c * SIDE + s], at(p, ss, cc), x
        )

    def x_copy(t, i):
        return remote(part.at[t, i], parts.at[t, x], x_send.at[t, i], x_recv.at[t, x], area, i)

    def halve(i, block):
        units = block.astype(jnp.int32)
        high = (units + 128) >> 8
        halves[i, :ROWS] = high.astype(F32).astype(BF16)
        halves[i, ROWS:] = (units - (high << 8)).astype(F32).astype(BF16)

    def product(i, sources):
        both = jnp.dot(halves[i], sources, preferred_element_type=F32)
        return (both[:ROWS] * 256.0 + both[ROWS:]) * (1.0 / UNITS)

    targets = [(ss, cc) for ss in far for cc in (c, 1 - c)] + [(s, 1 - c)]

    def early_copy(pp):
        return remote(early.at[pp], early_in.at[p], early_send.at[pp], early_recv.at[p], at(pp, s, c), x)

    lane = lax.broadcasted_iota(jnp.int32, (2 * SIDE, ROWS), 1).astype(F32)

    def one_hot(wanted, index):
        for q in range(PROJ):
            column = jnp.broadcast_to(wanted[:, q : q + 1], (2 * SIDE, ROWS))
            for b in range(DEPTH):
                pick[index, q * 2 * SIDE : (q + 1) * 2 * SIDE, b * ROWS : (b + 1) * ROWS] = jnp.where(
                    column == lane + float(b * ROWS), 1.0, 0.0
                ).astype(BF16)

    states = jnp.concatenate([held[p, DEPTH - 1 - b] for b in range(DEPTH)], axis=0)
    for pp in range(SIDE):
        one_hot(table[pp], pp)
        early[pp] = jnp.dot(pick[pp], states, preferred_element_type=F32).astype(BF16)

    loads[0].wait()
    loads[1].wait()
    def prepare(k):
        units = jnp.round(raw[:, k, :] * UNITS).astype(jnp.int32)
        high = (units + 128) >> 8
        both = jnp.concatenate([high, units - (high << 8)], axis=0).astype(F32).astype(BF16)
        moved = jnp.dot(both, moves[...], preferred_element_type=F32)
        w[k, :, :LONG] = (moved[:ROWS] * 256.0 + moved[ROWS:]).astype(jnp.int32).astype(jnp.int16)
        near_units = jnp.round(w_local[:, k * ROWS : (k + 1) * ROWS] * UNITS)
        w[k, :, LONG:] = near_units.astype(jnp.int32).astype(jnp.int16)

    def give(k):
        @pl.when(k != x)
        def _():
            w_copy(k).start()

    for k in range(PEERS // 2):
        prepare(k)

    pl.semaphore_wait(barrier, 2 * len(near) + len(every) + len(across))

    for pp in near:
        early_copy(pp).start()
    for k in range(PEERS):
        if k >= PEERS // 2:
            prepare(k)
        give(k)
    for pp in near:
        table_copy(pp).start()

    def foresee(t, is_second):
        for pp in every:
            if is_second and pp is not every[0]:
                arrive(held.at[pp, pl.ds(1, DEPTH - 1)], first_recv.at[pp])
            states = jnp.concatenate([held[pp, t + DEPTH - 1 - b] for b in range(1, DEPTH)], axis=0)
            older[pp] = jnp.dot(pick[pp, :, ROWS:], states, preferred_element_type=F32)

    def step(t, is_first):
        for pp in every:
            if is_first:
                if pp is not every[0]:
                    arrive(early_in.at[pp], early_recv.at[pp])
                    rows = early_in[pp].astype(F32)
                else:
                    rows = early[p].astype(F32)
            else:
                if pp is not every[0]:
                    arrive(held.at[pp, t + DEPTH - 1], hop1_recv.at[t, pp])
                rows = older[pp] + jnp.dot(
                    pick[pp, :, :ROWS], held[pp, t + DEPTH - 1], preferred_element_type=F32
                )
            for q in range(PROJ):
                mixed[pl.ds(q * SIDE + pp, 2 * SIDE, stride=MSG), :] = rows[q * 2 * SIDE : (q + 1) * 2 * SIDE]
        for a in range(2 * SIDE):
            msg[t, a] = mixed[a * MSG : (a + 1) * MSG, :].astype(BF16)
        for ss, cc in targets:
            hop2_copy(t, ss, cc).start()
        got[t, c * SIDE + s] = msg[t, s * 2 + c]
        if is_first:
            for pp in near:
                first_copy(pp).start()
            for pp in every:
                if pp is not every[0]:
                    arrive(tables.at[pp], table_recv.at[pp])
                one_hot(tables[pp], pp)
            halve(x, w[x])
        for ss in far:
            arrive(got.at[t, c * SIDE + ss], hop2_recv.at[t, c * SIDE + ss])
        for pp in every:
            arrive(got.at[t, (1 - c) * SIDE + pp], hop2_recv.at[t, (1 - c) * SIDE + pp])
        sources = jnp.concatenate([got[t].reshape(LONG, ROWS), held[p, t + DEPTH - 1]], axis=0)
        for i in across[1:] + across[:1] if is_first else across:
            if is_first:
                arrive(wg.at[i], w_recv.at[i])
                halve(i, wg[i])
            part[t, i] = product(i, sources).astype(BF16)
            x_copy(t, i).start()
        total = product(x, sources) + drive[...]
        for i in across:
            arrive(parts.at[t, i], x_recv.at[t, i])
            total += parts[t, i].astype(F32)
        old = rate[...]
        new = mask[...] * (old + pace[...] * (jnp.tanh(total) - old))
        return new

    def advance(t, is_first, is_second=False):
        new = step(t, is_first)
        rate[...] = new
        held[p, t + DEPTH] = new.astype(BF16)
        for pp in near:
            hop1_copy(t + 1, pp).start()
        foresee(t + 1, is_first)
        for ss, cc in targets:
            hop2_copy(t, ss, cc).wait_send()
        for i in across:
            x_copy(t, i).wait_send()
        if is_first:
            for pp in near:
                table_copy(pp).wait_send()
                early_copy(pp).wait_send()
            for i in across:
                w_copy(i).wait_send()
        else:
            for pp in near:
                if is_second:
                    first_copy(pp).wait_send()
                hop1_copy(t, pp).wait_send()

    advance(0, True)
    advance(1, False, True)

    @pl.loop(2, STEPS - 1)
    def _(t):
        advance(t, False)

    last = STEPS - 1
    out[...] = step(last, False)
    for pp in near:
        hop1_copy(last, pp).wait_send()
    for ss, cc in targets:
        hop2_copy(last, ss, cc).wait_send()
    for i in across:
        x_copy(last, i).wait_send()


def place_of_columns():
    place = np.zeros((2 * SIDE * SIDE * PROJ,), np.int32)
    for zz in range(SIDE):
        for yy in range(SIDE):
            for cc in range(2):
                for q in range(PROJ):
                    mid, src = (yy, zz) if cc == 0 else (SIDE + zz, yy)
                    place[((zz * SIDE + yy) * 2 + cc) * PROJ + q] = mid * MSG + q * SIDE + src
    return place


def local(history, drive, leak, w_local, w_long, sender_rows, delays, area_sizes):
    spread = jnp.asarray(place_of_columns()[:, None] == np.arange(LONG)[None, :], BF16)
    vmem = pl.BlockSpec(memory_space=pltpu.VMEM)
    hbm = pl.BlockSpec(memory_space=pl.ANY)
    dma = pltpu.SemaphoreType.DMA
    return pl.pallas_call(
        kernel,
        out_shape=jax.ShapeDtypeStruct((ROWS, ROWS), F32),
        in_specs=[vmem, vmem, vmem, pl.BlockSpec(memory_space=pltpu.SMEM), hbm, vmem, vmem, hbm, hbm],
        out_specs=vmem,
        scratch_shapes=[
            pltpu.VMEM((ROWS, ROWS), F32),
            pltpu.VMEM((SIDE, 2 * SIDE, ROWS), F32),
            pltpu.VMEM((SIDE, 2 * SIDE, ROWS), F32),
            pltpu.VMEM((SIDE, DEPTH + STEPS, ROWS, ROWS), BF16),
            pltpu.VMEM((SIDE, CODES, DEPTH * ROWS), BF16),
            pltpu.VMEM((SIDE, CODES, ROWS), F32),
            pltpu.VMEM((LONG, ROWS), F32),
            pltpu.VMEM((STEPS, 2 * SIDE, MSG, ROWS), BF16),
            pltpu.VMEM((STEPS, 2 * SIDE, MSG, ROWS), BF16),
            pltpu.VMEM((SIDE, CODES, ROWS), BF16),
            pltpu.VMEM((SIDE, CODES, ROWS), BF16),
            pltpu.VMEM((ROWS, PEERS, COLUMNS), F32),
            pltpu.VMEM((COLUMNS, LONG), BF16),
            pltpu.VMEM((PROJ, 1, ROWS), jnp.int32),
            pltpu.VMEM((PEERS, ROWS, LONG + ROWS), jnp.int16),
            pltpu.VMEM((PEERS, ROWS, LONG + ROWS), jnp.int16),
            pltpu.VMEM((PEERS, 2 * ROWS, LONG + ROWS), BF16),
            pltpu.VMEM((STEPS, PEERS, ROWS, ROWS), BF16),
            pltpu.VMEM((STEPS, PEERS, ROWS, ROWS), BF16),
            pltpu.VMEM((ROWS, ROWS), F32),
            pltpu.VMEM((ROWS, ROWS), F32),
            pltpu.VMEM((ROWS, ROWS), F32),
            dma((3,)), dma((SIDE,)), dma((SIDE,)), dma((SIDE,)), dma((SIDE,)), dma((SIDE,)), dma((SIDE,)), dma((PEERS,)), dma((PEERS,)),
            dma((STEPS, SIDE)), dma((STEPS, SIDE)), dma((STEPS, 2 * SIDE)), dma((STEPS, 2 * SIDE)),
            dma((STEPS, PEERS)), dma((STEPS, PEERS)),
        ],
        compiler_params=pltpu.CompilerParams(
            collective_id=0, has_side_effects=True, vmem_limit_bytes=60 * 1024 * 1024
        ),
        cost_estimate=pl.CostEstimate(flops=2 * 10**9, bytes_accessed=4 * 10**6, transcendentals=10**5),
    )(history, drive, leak.reshape(1, ROWS), area_sizes, sender_rows.transpose(2, 0, 1), delays, w_local, w_long, spread)


def solution(mesh):
    placed = (
        P(None, ("area", "nrn"), None),
        P(("area", "nrn"), None),
        P(("area", "nrn")),
        P(("area", "nrn"), None),
        P(("area", "nrn"), None, None),
        P(("area", "nrn"), None, None),
        P("area", None),
        P("area"),
    )
    return jax.shard_map(
        local, mesh=mesh, in_specs=placed, out_specs=P(("area", "nrn"), None), check_vma=False
    )
```
